512 devices in a mesh: row: 16 (over y, core), col: 32 (over z, x).
Axes of the slice: x: 4, y: 8, z: 8, core: 2. Of those that a mesh axis runs over, the one named last changes fastest.
Arguments:
- rhs_block: float32 [1024, 2048], P('row', 'col'), may hold values from -6 to 6
- diag_inverse: float32 [2048, 2048], P('col', 'row'), may hold values from -0.25 to 0.25
- panel: bfloat16 [2048, 196608], P(None, ('row', 'col')), may hold values from -0.125 to 0.125
- rhs_trail: float32 [1024, 196608], P(None, ('row', 'col')), may hold values from -6 to 6
Outputs:
- solved: float32 [1024, 2048], P('row', 'col')
- updated: float32 [1024, 196608], P(None, ('row', 'col'))
The draws below stay inside these ranges and needn't reach their ends.
All inputs are finite; a program needn't handle non-finite values.
Results may differ from the reference program's by a relative error of at most 0.0022.
Values may be sent and summed in bfloat16 or wider, within the bound.
No kernel may reach another device: no remote copies, remote signals or barrier semaphores. Data moves between devices by JAX's collectives and lax.ppermute only.
A program may use at most 64 MiB of HBM per device.

```python
import jax
import jax.numpy as jnp
from jax import lax

B = 2048
R = 1024
M = 196608


def with_spikes(entries, stream_key, source, target, shards_of, factor):
    def block_of(position):
        return (jnp.arange(entries.shape[position]) // (entries.shape[position] // shards_of)).reshape((-1,) + (1,) * (entries.ndim - 1 - position))

    near = jax.random.permutation(stream_key, shards_of)[block_of(target)]
    other_side = (block_of(target) + shards_of // 2) % shards_of
    return jnp.where((block_of(source) == near) | (block_of(source) == other_side), factor * entries, entries)


def block_levels(stream_key, shape, split, low, largest):
    level = 1.0
    for dim, blocks in split:
        draws = jax.random.uniform(jax.random.fold_in(jax.random.fold_in(stream_key, 6), dim), (blocks,), jnp.float32, low / len(split), largest / len(split))
        level = level * jnp.repeat(jnp.exp(draws), shape[dim] // blocks).reshape((-1,) + (1,) * (len(shape) - 1 - dim))
    return level


def normal_values(stream_key, extent, spread, bound, pieces=(), held_as=jnp.bfloat16):
    array = jax.random.normal(stream_key, extent, jnp.float32) * spread
    if len(pieces) > 0:
        array = block_levels(stream_key, extent, pieces, -0.22, 0.18) * array
    return jnp.clip(array, min=-bound, max=bound).astype(held_as)


def gaussian_with(stream_key, shape, width, limit, pieces, heavy, dtype=jnp.bfloat16):
    drawn = width * jax.random.normal(stream_key, shape, jnp.float32)
    if pieces:
        drawn = drawn * block_levels(stream_key, shape, pieces, -0.22, 0.18)
    return jnp.clip(with_spikes(drawn, jax.random.fold_in(stream_key, 3), *heavy), -limit, limit).astype(dtype)


def setup_inputs(seed: int = 0) -> dict:
    arg_keys = jax.random.split(jax.random.key(seed), 5)
    rhs_block = normal_values(arg_keys[0], (R, B), 1.0, 6.0, ((0, 16), (1, 32)), jnp.float32)
    diag_inverse = gaussian_with(arg_keys[1], (B, B), B ** -0.5, 0.25, ((0, 32), (1, 16)), (0, 1, 32, 2.75), jnp.float32)
    panel = normal_values(arg_keys[2], (B, M), B ** -0.5, 0.125, ((1, 512),))
    rhs_trail = normal_values(arg_keys[3], (R, M), 1.0, 6.0, ((1, 512),), jnp.float32)
    return {"rhs_block": rhs_block, "diag_inverse": diag_inverse, "panel": panel, "rhs_trail": rhs_trail}


def reference(rhs_block, diag_inverse, panel, rhs_trail):
    solved = jnp.dot(rhs_block, diag_inverse, preferred_element_type=jnp.float32, precision=lax.Precision.HIGHEST)
    solved_low = solved.astype(jnp.bfloat16)
    update = jnp.dot(solved_low, panel, preferred_element_type=jnp.float32)
    return solved, rhs_trail - update
```

```python
import functools

import jax
import jax.numpy as jnp
from jax import lax
from jax.experimental import pallas as pl
from jax.experimental.pallas import tpu as pltpu
from jax.sharding import PartitionSpec as P


def update_kernel(blocks_ref, panel_ref, trail_ref, out_ref):
    low = jnp.concatenate([blocks_ref[i] for i in range(blocks_ref.shape[0])], axis=1)
    out_ref[...] = trail_ref[...] - jnp.dot(low, panel_ref[...], preferred_element_type=jnp.float32)


def updated_trail(blocks, panel, trail, rows=256):
    count, total, width = blocks.shape
    columns = panel.shape[1]
    return pl.pallas_call(
        update_kernel,
        out_shape=jax.ShapeDtypeStruct(trail.shape, jnp.float32),
        grid=(total // rows,),
        in_specs=[
            pl.BlockSpec((count, rows, width), lambda i: (0, i, 0)),
            pl.BlockSpec((count * width, columns), lambda i: (0, 0)),
            pl.BlockSpec((rows, columns), lambda i: (i, 0)),
        ],
        out_specs=pl.BlockSpec((rows, columns), lambda i: (i, 0)),
        compiler_params=pltpu.CompilerParams(vmem_limit_bytes=32 * 1024 * 1024),
        cost_estimate=pl.CostEstimate(
            flops=2 * total * count * width * columns, bytes_accessed=9 * 1024 * 1024, transcendentals=0
        ),
    )(blocks, panel, trail)


def placed(tile, n_row, n_col):
    odd = lax.axis_index("col") % 2 == 1
    left, right = jnp.split(tile, 2, axis=1)
    same = [(r * n_col + c, c // 2 * n_col + 2 * r + c % 2) for r in range(n_row) for c in range(n_col)]
    other = [(r * n_col + c, c // 2 * n_col + 2 * r + 1 - c % 2) for r in range(n_row) for c in range(n_col)]
    a = lax.ppermute(jnp.where(odd, right, left), ("row", "col"), same)
    b = lax.ppermute(jnp.where(odd, left, right), ("row", "col"), other)
    return jnp.where(odd, jnp.concatenate([b, a]), jnp.concatenate([a, b]))


def local(n_row, n_col, rhs_block, diag_inverse, panel, rhs_trail):
    rows = lax.all_gather(rhs_block, "row", axis=0, tiled=True)
    partial = jnp.dot(rows, diag_inverse, preferred_element_type=jnp.float32, precision=lax.Precision.HIGHEST)
    height, width = partial.shape[0] // n_col, partial.shape[1]
    shares = lax.all_to_all(partial.reshape(n_col, height, width), "col", 0, 0, tiled=True)
    tile = jnp.sum(shares, axis=0)
    low = jnp.broadcast_to(tile.astype(jnp.bfloat16)[None], (n_col, height, width))
    band = lax.all_to_all(low, "col", 0, 0, tiled=True).reshape(n_col * height, width)
    blocks = lax.all_gather(band, "row", axis=0, tiled=False)
    return placed(tile, n_row, n_col), updated_trail(blocks, panel, rhs_trail)


def solution(mesh):
    return jax.shard_map(
        functools.partial(local, mesh.shape["row"], mesh.shape["col"]),
        mesh=mesh,
        in_specs=(
            P("row", "col"),
            P("col", "row"),
            P(None, ("row", "col")),
            P(None, ("row", "col")),
        ),
        out_specs=(P("row", "col"), P(None, ("row", "col"))),
        check_vma=False,
    )
```

```python
import functools

import jax
import jax.numpy as jnp
from jax import lax
from jax.experimental import pallas as pl
from jax.experimental.pallas import tpu as pltpu
from jax.sharding import Mesh, PartitionSpec as P

ROW = ("yf", "yn", "core")
COL = ("zf", "zn", "x")
FAR = ("yf", "zf")
NEAR = ("yn", "zn", "x")
SWAP = [(0, 1), (1, 0)]
TOP = 15.0


def vmem(mib):
    return pltpu.CompilerParams(vmem_limit_bytes=mib * 1024 * 1024)


def crossed(top, bottom):
    half = top.shape[1] // 2
    first = lax.broadcasted_iota(jnp.int32, top.shape, 1) < half
    return (
        jnp.where(first, top, pltpu.roll(bottom, half, 1)),
        jnp.where(first, pltpu.roll(top, half, 1), bottom),
    )


def partial_kernel(rhs_ref, band_ref, out_ref):
    band = jnp.concatenate([band_ref[i] for i in range(band_ref.shape[0])], axis=1)
    partial = jnp.dot(
        rhs_ref[...], band, preferred_element_type=jnp.float32, precision=lax.Precision.HIGHEST
    )
    largest = jnp.maximum(jnp.max(jnp.abs(partial), axis=(0, 1), keepdims=True), 2.0**-100)
    power = jnp.ceil(jnp.log2(largest))
    partial = partial * jnp.exp2(TOP - power)
    height = partial.shape[0] // 2
    for j in range(partial.shape[1] // 128):
        both = partial[:, 128 * j : 128 * (j + 1)]
        out_ref[2 * j, :height], out_ref[2 * j + 1, :height] = crossed(both[:height], both[height:])
    out_ref[:, height:] = jnp.broadcast_to(power[None], (out_ref.shape[0], 8, 128))


def partial_blocks(rhs, band):
    count, _, width = band.shape
    blocks = count * width // 64
    return pl.pallas_call(
        partial_kernel,
        out_shape=jax.ShapeDtypeStruct((blocks, rhs.shape[0] // 2 + 8, 128), jnp.float32),
        compiler_params=vmem(8),
    )(rhs, band)


def sum_kernel(shares_ref, solved_ref, low_ref):
    height, half = shares_ref.shape[1] - 8, shares_ref.shape[2] // 2
    scale = jnp.exp2(shares_ref[:, height:] - TOP)
    total = jnp.concatenate(
        [jnp.sum(shares_ref[:, i : i + 8] * scale, axis=0) for i in range(0, height, 8)], axis=0
    )
    solved_ref[:height] = total[:, :half]
    solved_ref[height:] = pltpu.roll(total, half, 1)[:, :half]
    low_ref[...] = jnp.broadcast_to(total.astype(jnp.bfloat16)[None], low_ref.shape)


def summed(shares, copies):
    height, width = shares.shape[1] - 8, shares.shape[2]
    return pl.pallas_call(
        sum_kernel,
        out_shape=(
            jax.ShapeDtypeStruct((2 * height, width // 2), jnp.float32),
            jax.ShapeDtypeStruct((copies, height, width), jnp.bfloat16),
        ),
        compiler_params=vmem(8),
    )(shares)


def stripes_kernel(core_ref, tiles_ref, panel_ref, trail_ref, *rest):
    yn = pl.program_id(0) if tiles_ref.shape[0] > 1 else 0
    _, near, far_y, far_z, _, _ = tiles_ref.shape
    rows = []
    for y in range(far_y):
        pairs = [
            crossed(tiles_ref[yn, i, y, z], tiles_ref[yn, i + 1, y, z])
            for z in range(far_z)
            for i in range(0, near, 2)
        ]
        rows += [jnp.concatenate([p[h] for p in pairs], axis=1) for h in range(2)]
    update = jnp.dot(jnp.concatenate(rows, axis=0), panel_ref[...], preferred_element_type=jnp.float32)
    out_ref = rest[-1]
    out_ref[...] = trail_ref[...] - update.reshape(out_ref.shape)


def updated_stripes(tiles, panel, trail, core, done=None):
    near_y, near, far_y, far_z, height, width = tiles.shape
    columns = panel.shape[1]
    stripe = pl.BlockSpec((far_y, 1, 1, 2 * height, columns), lambda i, core: (0, i, core[0], 0, 0))
    whole = pl.BlockSpec(memory_space=pltpu.VMEM)
    one = pl.BlockSpec((1,) + tiles.shape[1:], lambda i, core: (i, 0, 0, 0, 0, 0))
    flops = 2 * near_y * far_y * 2 * height * panel.shape[0] * columns
    return pl.pallas_call(
        stripes_kernel,
        out_shape=jax.ShapeDtypeStruct(trail.shape, jnp.float32),
        grid_spec=pltpu.PrefetchScalarGridSpec(
            num_scalar_prefetch=1,
            grid=(near_y,),
            in_specs=[whole, whole, stripe] if done is None else [one, whole, stripe, pl.BlockSpec(memory_space=pl.ANY)],
            out_specs=stripe,
        ),
        input_output_aliases={} if done is None else {4: 0},
        compiler_params=vmem(20),
        cost_estimate=pl.CostEstimate(flops=flops, bytes_accessed=5 * 1024 * 1024, transcendentals=0),
    )(core, tiles, panel, trail, *([] if done is None else [done]))


def local(size, rhs_block, diag_inverse, panel, rhs_trail):
    band = lax.all_gather(diag_inverse, ROW, axis=0, tiled=False)
    blocks = partial_blocks(rhs_block, band).astype(jnp.float16)
    shares = lax.all_to_all(blocks, COL, 0, 0, tiled=True)
    solved, low = summed(shares.astype(jnp.float32), size["yf"] * size["zf"])
    far = lax.all_to_all(low, FAR, 0, 0, tiled=True)
    copies = size["yn"] * size["zn"] * size["x"]
    near = lax.all_to_all(jnp.broadcast_to(far[None], (copies,) + far.shape), NEAR, 0, 0, tiled=True)
    tiles = near.reshape(size["yn"], size["zn"] * size["x"], size["yf"], size["zf"], *far.shape[1:])
    other = lax.ppermute(tiles, "core", SWAP)
    core = lax.axis_index("core").reshape(1)
    trail = rhs_trail.reshape(size["yf"], size["yn"], 2, 2 * far.shape[1], rhs_trail.shape[1])
    done = updated_stripes(tiles, panel, trail, core)
    done = updated_stripes(other, panel, trail, 1 - core, done)
    return solved, done.reshape(rhs_trail.shape)


def solution(mesh):
    split = Mesh(mesh.devices.reshape(4, 2, 2, 4, 2, 4), ROW + COL)
    return jax.shard_map(
        functools.partial(local, dict(split.shape)),
        mesh=split,
        in_specs=(P(ROW, COL), P(COL, ROW), P(None, ROW + COL), P(None, ROW + COL)),
        out_specs=(P(ROW, COL), P(None, ROW + COL)),
        check_vma=False,
    )
```

```python
import functools

import jax
import jax.numpy as jnp
from jax import lax
from jax.experimental import pallas as pl
from jax.experimental.pallas import tpu as pltpu
from jax.sharding import Mesh, PartitionSpec as P

ROW = ("yf", "yn", "core")
COL = ("zf", "zn", "xf", "xn")
FAR = ("yf", "zf", "xf")
NEAR = ("yn", "zn", "xn")
SWAP = [(0, 1), (1, 0)]
TOP = 15.0


def vmem(mib):
    return pltpu.CompilerParams(vmem_limit_bytes=mib * 1024 * 1024)


def crossed(top, bottom):
    half = top.shape[1] // 2
    first = lax.broadcasted_iota(jnp.int32, top.shape, 1) < half
    return (
        jnp.where(first, top, pltpu.roll(bottom, half, 1)),
        jnp.where(first, pltpu.roll(top, half, 1), bottom),
    )


def partial_kernel(rhs_ref, band_ref, out_ref):
    band = jnp.concatenate([band_ref[i] for i in range(band_ref.shape[0])], axis=1)
    partial = jnp.dot(
        rhs_ref[...], band, preferred_element_type=jnp.float32, precision=lax.Precision.HIGHEST
    )
    largest = jnp.maximum(jnp.max(jnp.abs(partial), axis=(0, 1), keepdims=True), 2.0**-100)
    power = jnp.ceil(jnp.log2(largest))
    partial = partial * jnp.exp2(TOP - power)
    height = partial.shape[0] // 2
    for j in range(partial.shape[1] // 128):
        both = partial[:, 128 * j : 128 * (j + 1)]
        out_ref[2 * j, :height], out_ref[2 * j + 1, :height] = crossed(both[:height], both[height:])
    out_ref[:, height:] = jnp.broadcast_to(power[None], (out_ref.shape[0], 8, 128))


def partial_blocks(rhs, band):
    count, _, width = band.shape
    blocks = count * width // 64
    return pl.pallas_call(
        partial_kernel,
        out_shape=jax.ShapeDtypeStruct((blocks, rhs.shape[0] // 2 + 8, 128), jnp.float32),
        compiler_params=vmem(8),
    )(rhs, band)


def sum_kernel(shares_ref, solved_ref, low_ref):
    height, half = shares_ref.shape[1] - 8, shares_ref.shape[2] // 2
    scale = jnp.exp2(shares_ref[:, height:] - TOP)
    total = jnp.concatenate(
        [jnp.sum(shares_ref[:, i : i + 8] * scale, axis=0) for i in range(0, height, 8)], axis=0
    )
    solved_ref[:height] = total[:, :half]
    solved_ref[height:] = pltpu.roll(total, half, 1)[:, :half]
    low_ref[...] = jnp.broadcast_to(total.astype(jnp.bfloat16)[None], low_ref.shape)


def summed(shares, copies):
    height, width = shares.shape[1] - 8, shares.shape[2]
    return pl.pallas_call(
        sum_kernel,
        out_shape=(
            jax.ShapeDtypeStruct((2 * height, width // 2), jnp.float32),
            jax.ShapeDtypeStruct((copies, height, width), jnp.bfloat16),
        ),
        compiler_params=vmem(8),
    )(shares)


def stripes_kernel(core_ref, tiles_ref, panel_ref, trail_ref, *rest):
    yn = pl.program_id(0) if tiles_ref.shape[0] > 1 else 0
    _, near_z, _, far_y, far_z, far_x, _, _ = tiles_ref.shape
    rows = []
    for y in range(far_y):
        pairs = [
            crossed(tiles_ref[yn, n, 0, y, z, x], tiles_ref[yn, n, 1, y, z, x])
            for z in range(far_z)
            for n in range(near_z)
            for x in range(far_x)
        ]
        rows += [jnp.concatenate([p[h] for p in pairs], axis=1) for h in range(2)]
    update = jnp.dot(jnp.concatenate(rows, axis=0), panel_ref[...], preferred_element_type=jnp.float32)
    out_ref = rest[-1]
    out_ref[...] = trail_ref[...] - update.reshape(out_ref.shape)


def updated_stripes(tiles, panel, trail, core, done=None):
    near_y, far_y, height = tiles.shape[0], tiles.shape[3], tiles.shape[6]
    columns = panel.shape[1]
    stripe = pl.BlockSpec((far_y, 1, 1, 2 * height, columns), lambda i, core: (0, i, core[0], 0, 0))
    whole = pl.BlockSpec(memory_space=pltpu.VMEM)
    one = pl.BlockSpec((1,) + tiles.shape[1:], lambda i, core: (i,) + (0,) * 7)
    flops = 2 * near_y * far_y * 2 * height * panel.shape[0] * columns
    return pl.pallas_call(
        stripes_kernel,
        out_shape=jax.ShapeDtypeStruct(trail.shape, jnp.float32),
        grid_spec=pltpu.PrefetchScalarGridSpec(
            num_scalar_prefetch=1,
            grid=(near_y,),
            in_specs=[whole, whole, stripe] if done is None else [one, whole, stripe, pl.BlockSpec(memory_space=pl.ANY)],
            out_specs=stripe,
        ),
        input_output_aliases={} if done is None else {4: 0},
        compiler_params=vmem(20),
        cost_estimate=pl.CostEstimate(flops=flops, bytes_accessed=5 * 1024 * 1024, transcendentals=0),
    )(core, tiles, panel, trail, *([] if done is None else [done]))


def cubes(size):
    count_y, count_z, count_x = 2 * size["yf"], 2 * size["zf"], 2 * size["xf"]

    def device(y, core, z, x):
        return ((y % count_y * size["core"] + core) * count_z + z % count_z) * count_x + x % count_x

    def place(corner, parity, core):
        return corner + (2 - parity if core else parity)

    return [
        [
            device(place(y, a, core), core, place(z, b, core), place(x, c, core))
            for a in range(2)
            for b in range(2)
            for c in range(2)
        ]
        for y in range(0, count_y, 2)
        for core in range(size["core"])
        for z in range(0, count_z, 2)
        for x in range(0, count_x, 2)
    ]


def local(size, rhs_block, diag_inverse, panel, rhs_trail):
    band = lax.all_gather(diag_inverse, ROW, axis=0, tiled=False)
    blocks = partial_blocks(rhs_block, band).astype(jnp.float16)
    shares = lax.all_to_all(blocks, COL, 0, 0, tiled=True)
    solved, low = summed(shares.astype(jnp.float32), size["yf"] * size["zf"] * size["xf"])
    far = lax.all_to_all(low, FAR, 0, 0, tiled=True)
    copies = size["yn"] * size["zn"] * size["xn"]
    near = lax.all_to_all(
        jnp.broadcast_to(far[None], (copies,) + far.shape), ROW + COL, 0, 0, tiled=True, axis_index_groups=cubes(size)
    )
    tiles = near.reshape(tuple(size[a] for a in NEAR + FAR) + far.shape[1:])
    other = lax.ppermute(tiles, "core", SWAP)
    core = lax.axis_index("core").reshape(1)
    trail = rhs_trail.reshape(size["yf"], size["yn"], 2, 2 * far.shape[1], rhs_trail.shape[1])
    done = updated_stripes(tiles, panel, trail, core)
    done = updated_stripes(other, panel, trail, 1 - core, done)
    return solved, done.reshape(rhs_trail.shape)


def solution(mesh):
    split = Mesh(mesh.devices.reshape(4, 2, 2, 4, 2, 2, 2), ROW + COL)
    return jax.shard_map(
        functools.partial(local, dict(split.shape)),
        mesh=split,
        in_specs=(P(ROW, COL), P(COL, ROW), P(None, ROW + COL), P(None, ROW + COL)),
        out_specs=(P(ROW, COL), P(None, ROW + COL)),
        check_vma=False,
    )
```

```python
import functools

import jax
import jax.numpy as jnp
from jax import lax
from jax.experimental import pallas as pl
from jax.experimental.pallas import tpu as pltpu
from jax.sharding import Mesh, PartitionSpec as P

ROW = ("yf", "yn", "core")
COL = ("zf", "zn", "xf", "xn")
FAR = ("zf", "yf", "xf")
NEAR = ("zn", "yn", "xn")
SWAP = [(0, 1), (1, 0)]
TOP = 15.0


def vmem(mib):
    return pltpu.CompilerParams(vmem_limit_bytes=mib * 1024 * 1024)


def crossed(top, bottom):
    half = top.shape[1] // 2
    first = lax.broadcasted_iota(jnp.int32, top.shape, 1) < half
    return (
        jnp.where(first, top, pltpu.roll(bottom, half, 1)),
        jnp.where(first, pltpu.roll(top, half, 1), bottom),
    )


def partial_kernel(rhs_ref, mine_ref, other_ref, core_ref, out_ref):
    count, height, half = rhs_ref.shape[0], rhs_ref.shape[1], rhs_ref.shape[2] // 2
    rows = []
    for i in range(count):
        both = rhs_ref[i]
        rows += [both[:, :half], pltpu.roll(both, half, 1)[:, :half]]
    first = core_ref[0] == 0
    mine, other = mine_ref[...], other_ref[...]
    inverse = jnp.concatenate([jnp.where(first, mine, other), jnp.where(first, other, mine)], axis=1)
    partial = jnp.dot(
        jnp.concatenate(rows, axis=0), inverse, preferred_element_type=jnp.float32, precision=lax.Precision.HIGHEST
    )
    largest = jnp.maximum(jnp.max(jnp.abs(partial), axis=(0, 1), keepdims=True), 2.0**-100)
    power = jnp.ceil(jnp.log2(largest))
    partial = partial * jnp.exp2(TOP - power)
    block = 0
    for i in range(count):
        for j in range(partial.shape[1] // 128):
            both = partial[2 * height * i : 2 * height * (i + 1), 128 * j : 128 * (j + 1)]
            out_ref[block, :height], out_ref[block + 1, :height] = crossed(both[:height], both[height:])
            block += 2
    out_ref[:, height:] = jnp.broadcast_to(power[None], (out_ref.shape[0], 8, 128))


def partial_blocks(rhs, mine, other, core):
    count, height, _ = rhs.shape
    whole = pl.BlockSpec(memory_space=pltpu.VMEM)
    return pl.pallas_call(
        partial_kernel,
        out_shape=jax.ShapeDtypeStruct((count * 2 * mine.shape[1] // 64, height + 8, 128), jnp.float32),
        in_specs=[whole, whole, whole, pl.BlockSpec(memory_space=pltpu.SMEM)],
        compiler_params=vmem(8),
    )(rhs, mine, other, core)


def sum_kernel(shares_ref, panel_ref, trail_ref, solved_ref, low_ref):
    height, half = shares_ref.shape[1] - 8, shares_ref.shape[2] // 2
    scale = jnp.exp2(shares_ref[:, height:] - TOP)
    total = jnp.concatenate(
        [jnp.sum(shares_ref[:, i : i + 8] * scale, axis=0) for i in range(0, height, 8)], axis=0
    )
    solved_ref[:height] = total[:, :half]
    solved_ref[height:] = pltpu.roll(total, half, 1)[:, :half]
    low_ref[...] = jnp.broadcast_to(total.astype(jnp.bfloat16)[None], low_ref.shape)


def summed(shares, copies, panel, trail):
    height, width = shares.shape[1] - 8, shares.shape[2]
    return pl.pallas_call(
        sum_kernel,
        out_shape=(
            jax.ShapeDtypeStruct((2 * height, width // 2), jnp.float32),
            jax.ShapeDtypeStruct((copies, height, width), jnp.bfloat16),
        ),
        compiler_params=vmem(8),
    )(shares, panel, trail)


def stripes_kernel(core_ref, tiles_ref, panel_ref, trail_ref, *rest):
    yn = pl.program_id(0) if tiles_ref.shape[0] > 1 else 0
    _, near_z, _, far_y, far_z, far_x, _, _ = tiles_ref.shape
    rows = []
    for y in range(far_y):
        pairs = [
            crossed(tiles_ref[yn, n, 0, y, z, x], tiles_ref[yn, n, 1, y, z, x])
            for z in range(far_z)
            for n in range(near_z)
            for x in range(far_x)
        ]
        rows += [jnp.concatenate([p[h] for p in pairs], axis=1) for h in range(2)]
    update = jnp.dot(jnp.concatenate(rows, axis=0), panel_ref[...], preferred_element_type=jnp.float32)
    out_ref = rest[-1]
    out_ref[...] = trail_ref[...] - update.reshape(out_ref.shape)


def updated_stripes(tiles, panel, trail, core, done=None):
    near_y, far_y, height = tiles.shape[0], tiles.shape[3], tiles.shape[6]
    columns = panel.shape[1]
    stripe = pl.BlockSpec((far_y, 1, 1, 2 * height, columns), lambda i, core: (0, i, core[0], 0, 0))
    whole = pl.BlockSpec(memory_space=pltpu.VMEM)
    one = pl.BlockSpec((1,) + tiles.shape[1:], lambda i, core: (i,) + (0,) * 7)
    flops = 2 * near_y * far_y * 2 * height * panel.shape[0] * columns
    return pl.pallas_call(
        stripes_kernel,
        out_shape=jax.ShapeDtypeStruct(trail.shape, jnp.float32),
        grid_spec=pltpu.PrefetchScalarGridSpec(
            num_scalar_prefetch=1,
            grid=(near_y,),
            in_specs=[whole, whole, stripe] if done is None else [one, whole, stripe, pl.BlockSpec(memory_space=pl.ANY)],
            out_specs=stripe,
        ),
        input_output_aliases={} if done is None else {4: 0},
        compiler_params=vmem(20),
        cost_estimate=pl.CostEstimate(flops=flops, bytes_accessed=5 * 1024 * 1024, transcendentals=0),
    )(core, tiles, panel, trail, *([] if done is None else [done]))


def cubes(size):
    count_y, count_z, count_x = 2 * size["yf"], 2 * size["zf"], 2 * size["xf"]

    def device(y, core, z, x):
        return ((y % count_y * size["core"] + core) * count_z + z % count_z) * count_x + x % count_x

    def place(corner, parity, core):
        return corner + (2 - parity if core else parity)

    return [
        [
            device(place(y, b, core), core, place(z, a, core), place(x, c, core))
            for a in range(2)
            for b in range(2)
            for c in range(2)
        ]
        for y in range(0, count_y, 2)
        for core in range(size["core"])
        for z in range(0, count_z, 2)
        for x in range(0, count_x, 2)
    ]


def local(size, rhs_block, diag_inverse, panel, rhs_trail):
    core = lax.axis_index("core").reshape(1)
    other_inverse = lax.ppermute(diag_inverse, "core", SWAP)
    half, count_y, count_z = rhs_block.shape[0] // 2, size["yf"] * size["yn"], size["zf"] * size["zn"]
    rows = jnp.concatenate([rhs_block[:half], rhs_block[half:]], axis=1)
    rows = lax.all_to_all(jnp.broadcast_to(rows[None], (count_y,) + rows.shape), ("yf", "yn"), 0, 0, tiled=True)
    blocks = partial_blocks(rows, diag_inverse, other_inverse, core).astype(jnp.float16)
    shares = lax.all_to_all(blocks, COL, 0, 0, tiled=True)
    trail = rhs_trail.reshape(size["zf"], size["zn"], 2, 2 * half, rhs_trail.shape[1])
    solved, low = summed(shares.astype(jnp.float32), size["yf"] * size["zf"] * size["xf"], panel, trail)
    count_x = size["xf"] * size["xn"]
    swapped = [
        (((y * 2 + k) * count_z + z) * count_x + x, ((z * 2 + k) * count_y + y) * count_x + x)
        for y in range(count_y)
        for k in range(2)
        for z in range(count_z)
        for x in range(count_x)
    ]
    solved = lax.ppermute(solved, ROW + COL, swapped)
    far, solved = lax.optimization_barrier((lax.all_to_all(low, FAR, 0, 0, tiled=True), solved))
    copies = size["yn"] * size["zn"] * size["xn"]
    near = lax.all_to_all(
        jnp.broadcast_to(far[None], (copies,) + far.shape), ROW + COL, 0, 0, tiled=True, axis_index_groups=cubes(size)
    )
    tiles = near.reshape(tuple(size[a] for a in NEAR + FAR) + far.shape[1:])
    other = lax.ppermute(tiles, "core", SWAP)
    done = updated_stripes(tiles, panel, trail, core)
    done = updated_stripes(other, panel, trail, 1 - core, done)
    return solved, done.reshape(rhs_trail.shape)


def solution(mesh):
    split = Mesh(mesh.devices.reshape(4, 2, 2, 4, 2, 2, 2), ROW + COL)
    return jax.shard_map(
        functools.partial(local, dict(split.shape)),
        mesh=split,
        in_specs=(P(ROW, COL), P(COL, ROW), P(None, ROW + COL), P(None, ROW + COL)),
        out_specs=(P(ROW, COL), P(None, ROW + COL)),
        check_vma=False,
    )
```

```python
import functools

import jax
import jax.numpy as jnp
from jax import lax
from jax.experimental import pallas as pl
from jax.experimental.pallas import tpu as pltpu
from jax.sharding import Mesh, PartitionSpec as P

ROW = ("yf", "yn", "core")
COL = ("zf", "zn", "xf", "xn")
FAR = ("zf", "yf", "xf")
NEAR = ("zn", "yn", "xn")
SWAP = [(0, 1), (1, 0)]
TOP = 15.0


def vmem(mib):
    return pltpu.CompilerParams(vmem_limit_bytes=mib * 1024 * 1024)


def crossed(top, bottom):
    half = top.shape[1] // 2
    first = lax.broadcasted_iota(jnp.int32, top.shape, 1) < half
    return (
        jnp.where(first, top, pltpu.roll(bottom, half, 1)),
        jnp.where(first, pltpu.roll(top, half, 1), bottom),
    )


def partial_kernel(rhs_ref, mine_ref, other_ref, core_ref, out_ref):
    count, height, half = rhs_ref.shape[0], rhs_ref.shape[1], rhs_ref.shape[2] // 2
    rows = []
    for i in range(count):
        both = rhs_ref[i]
        rows += [both[:, :half], pltpu.roll(both, half, 1)[:, :half]]
    first = core_ref[0] == 0
    mine, other = mine_ref[...], other_ref[...]
    inverse = jnp.concatenate([jnp.where(first, mine, other), jnp.where(first, other, mine)], axis=1)
    partial = jnp.dot(
        jnp.concatenate(rows, axis=0), inverse, preferred_element_type=jnp.float32, precision=lax.Precision.HIGHEST
    )
    largest = jnp.maximum(jnp.max(jnp.abs(partial), axis=(0, 1), keepdims=True), 2.0**-100)
    power = jnp.ceil(jnp.log2(largest))
    partial = partial * jnp.exp2(TOP - power)
    block = 0
    for i in range(count):
        for j in range(partial.shape[1] // 128):
            both = partial[2 * height * i : 2 * height * (i + 1), 128 * j : 128 * (j + 1)]
            out_ref[block, :height], out_ref[block + 1, :height] = crossed(both[:height], both[height:])
            block += 2
    out_ref[:, height:] = jnp.broadcast_to(power[None], (out_ref.shape[0], 8, 128))


def partial_blocks(rhs, mine, other, core):
    count, height, _ = rhs.shape
    whole = pl.BlockSpec(memory_space=pltpu.VMEM)
    return pl.pallas_call(
        partial_kernel,
        out_shape=jax.ShapeDtypeStruct((count * 2 * mine.shape[1] // 64, height + 8, 128), jnp.float32),
        in_specs=[whole, whole, whole, pl.BlockSpec(memory_space=pltpu.SMEM)],
        compiler_params=vmem(8),
    )(rhs, mine, other, core)


def sum_kernel(shares_ref, panel_ref, trail_ref, solved_ref, low_ref):
    height, half = shares_ref.shape[1] - 8, shares_ref.shape[2] // 2
    scale = jnp.exp2(shares_ref[:, height:] - TOP)
    total = jnp.concatenate(
        [jnp.sum(shares_ref[:, i : i + 8] * scale, axis=0) for i in range(0, height, 8)], axis=0
    )
    solved_ref[:height] = total[:, :half]
    solved_ref[height:] = pltpu.roll(total, half, 1)[:, :half]
    low_ref[...] = jnp.broadcast_to(total.astype(jnp.bfloat16)[None], low_ref.shape)


def summed(shares, copies, panel, trail):
    height, width = shares.shape[1] - 8, shares.shape[2]
    return pl.pallas_call(
        sum_kernel,
        out_shape=(
            jax.ShapeDtypeStruct((2 * height, width // 2), jnp.float32),
            jax.ShapeDtypeStruct((copies, height, width), jnp.bfloat16),
        ),
        compiler_params=vmem(8),
    )(shares, panel, trail)


def stripes_kernel(core_ref, tiles_ref, panel_ref, trail_ref, passed_ref, out_ref, *rest):
    yn = pl.program_id(0)
    _, near_z, _, far_y, far_z, far_x, _, _ = tiles_ref.shape
    rows = []
    for y in range(far_y):
        pairs = [
            crossed(tiles_ref[yn, n, 0, y, z, x], tiles_ref[yn, n, 1, y, z, x])
            for z in range(far_z)
            for n in range(near_z)
            for x in range(far_x)
        ]
        rows += [jnp.concatenate([p[h] for p in pairs], axis=1) for h in range(2)]
    update = jnp.dot(jnp.concatenate(rows, axis=0), panel_ref[...], preferred_element_type=jnp.float32)
    out_ref[:, 0, 0] = trail_ref[:, yn, core_ref[0]] - update.reshape(far_y, -1, update.shape[1])
    for solved_ref in rest:
        solved_ref[...] = passed_ref[...]


def updated_stripes(tiles, panel, trail, core, solved=None, done=None):
    near_y, far_y, height = tiles.shape[0], tiles.shape[3], tiles.shape[6]
    columns = panel.shape[1]
    stripe = pl.BlockSpec((far_y, 1, 1, 2 * height, columns), lambda i, core: (0, i, core[0], 0, 0))
    whole = pl.BlockSpec(memory_space=pltpu.VMEM)
    flops = 2 * near_y * far_y * 2 * height * panel.shape[0] * columns
    out = jax.ShapeDtypeStruct(trail.shape, jnp.float32)
    block = None if solved is None else pl.BlockSpec(solved.shape, lambda i, core: (0, 0))
    return pl.pallas_call(
        stripes_kernel,
        out_shape=out if solved is None else (out, jax.ShapeDtypeStruct(solved.shape, solved.dtype)),
        grid_spec=pltpu.PrefetchScalarGridSpec(
            num_scalar_prefetch=1,
            grid=(near_y,),
            in_specs=[whole, whole, whole, pl.BlockSpec(memory_space=pl.ANY) if solved is None else block],
            out_specs=stripe if solved is None else (stripe, block),
        ),
        input_output_aliases={4: 0} if solved is None else {},
        compiler_params=vmem(20),
        cost_estimate=pl.CostEstimate(flops=flops, bytes_accessed=5 * 1024 * 1024, transcendentals=0),
    )(core, tiles, panel, trail, done if solved is None else solved)


def cubes(size):
    count_y, count_z, count_x = 2 * size["yf"], 2 * size["zf"], 2 * size["xf"]

    def device(y, core, z, x):
        return ((y % count_y * size["core"] + core) * count_z + z % count_z) * count_x + x % count_x

    def place(corner, parity, core):
        return corner + (2 - parity if core else parity)

    return [
        [
            device(place(y, b, core), core, place(z, a, core), place(x, c, core))
            for a in range(2)
            for b in range(2)
            for c in range(2)
        ]
        for y in range(0, count_y, 2)
        for core in range(size["core"])
        for z in range(0, count_z, 2)
        for x in range(0, count_x, 2)
    ]


def local(size, rhs_block, diag_inverse, panel, rhs_trail):
    core = lax.axis_index("core").reshape(1)
    other_inverse = lax.ppermute(diag_inverse, "core", SWAP)
    half, count_y, count_z = rhs_block.shape[0] // 2, size["yf"] * size["yn"], size["zf"] * size["zn"]
    rows = jnp.concatenate([rhs_block[:half], rhs_block[half:]], axis=1)
    rows = lax.all_to_all(jnp.broadcast_to(rows[None], (count_y,) + rows.shape), ("yf", "yn"), 0, 0, tiled=True)
    blocks = partial_blocks(rows, diag_inverse, other_inverse, core).astype(jnp.float16)
    shares = lax.all_to_all(blocks, COL, 0, 0, tiled=True)
    trail = rhs_trail.reshape(size["zf"], size["zn"], 2, 2 * half, rhs_trail.shape[1])
    solved, low = summed(shares.astype(jnp.float32), size["yf"] * size["zf"] * size["xf"], panel, trail)
    count_x = size["xf"] * size["xn"]
    swapped = [
        (((y * 2 + k) * count_z + z) * count_x + x, ((z * 2 + k) * count_y + y) * count_x + x)
        for y in range(count_y)
        for k in range(2)
        for z in range(count_z)
        for x in range(count_x)
    ]
    solved = lax.ppermute(solved, ROW + COL, swapped)
    far, solved = lax.optimization_barrier((lax.all_to_all(low, FAR, 0, 0, tiled=True), solved))
    copies = size["yn"] * size["zn"] * size["xn"]
    near = lax.all_to_all(
        jnp.broadcast_to(far[None], (copies,) + far.shape), ROW + COL, 0, 0, tiled=True, axis_index_groups=cubes(size)
    )
    tiles = near.reshape(tuple(size[a] for a in NEAR + FAR) + far.shape[1:])
    other = lax.ppermute(tiles, "core", SWAP)
    done, solved = updated_stripes(tiles, panel, trail, core, solved=solved)
    done = updated_stripes(other, panel, trail, 1 - core, done=done)
    return solved, done.reshape(rhs_trail.shape)


def solution(mesh):
    split = Mesh(mesh.devices.reshape(4, 2, 2, 4, 2, 2, 2), ROW + COL)
    return jax.shard_map(
        functools.partial(local, dict(split.shape)),
        mesh=split,
        in_specs=(P(ROW, COL), P(COL, ROW), P(None, ROW + COL), P(None, ROW + COL)),
        out_specs=(P(ROW, COL), P(None, ROW + COL)),
        check_vma=False,
    )
```

```python
import functools

import jax
import jax.numpy as jnp
from jax import lax
from jax.experimental import pallas as pl
from jax.experimental.pallas import tpu as pltpu
from jax.sharding import Mesh, PartitionSpec as P

ROW = ("yf", "yn", "core")
COL = ("zf", "zn", "xf", "xn")
FAR = ("zf", "yf", "xf")
NEAR = ("zn", "yn", "xn")
SWAP = [(0, 1), (1, 0)]
TOP = 15.0


def vmem(mib):
    return pltpu.CompilerParams(vmem_limit_bytes=mib * 1024 * 1024)


def crossed(top, bottom):
    half = top.shape[1] // 2
    first = lax.broadcasted_iota(jnp.int32, top.shape, 1) < half
    return (
        jnp.where(first, top, pltpu.roll(bottom, half, 1)),
        jnp.where(first, pltpu.roll(top, half, 1), bottom),
    )


def partial_kernel(rhs_ref, mine_ref, other_ref, core_ref, out_ref):
    count, height, half = rhs_ref.shape[0], rhs_ref.shape[1], rhs_ref.shape[2] // 2
    rows = []
    for i in range(count):
        both = rhs_ref[i]
        rows += [both[:, :half], pltpu.roll(both, half, 1)[:, :half]]
    first = core_ref[0] == 0
    mine, other = mine_ref[...], other_ref[...]
    inverse = jnp.concatenate([jnp.where(first, mine, other), jnp.where(first, other, mine)], axis=1)
    partial = jnp.dot(
        jnp.concatenate(rows, axis=0), inverse, preferred_element_type=jnp.float32, precision=lax.Precision.HIGHEST
    )
    largest = jnp.maximum(jnp.max(jnp.abs(partial), axis=(0, 1), keepdims=True), 2.0**-100)
    power = jnp.ceil(jnp.log2(largest))
    partial = partial * jnp.exp2(TOP - power)
    block = 0
    for i in range(count):
        for j in range(partial.shape[1] // 128):
            both = partial[2 * height * i : 2 * height * (i + 1), 128 * j : 128 * (j + 1)]
            out_ref[block, :height], out_ref[block + 1, :height] = crossed(both[:height], both[height:])
            block += 2
    out_ref[:, height:] = jnp.broadcast_to(power[None], (out_ref.shape[0], 8, 128))


def partial_blocks(rhs, mine, other, core):
    count, height, _ = rhs.shape
    whole = pl.BlockSpec(memory_space=pltpu.VMEM)
    return pl.pallas_call(
        partial_kernel,
        out_shape=jax.ShapeDtypeStruct((count * 2 * mine.shape[1] // 64, height + 8, 128), jnp.float32),
        in_specs=[whole, whole, whole, pl.BlockSpec(memory_space=pltpu.SMEM)],
        compiler_params=vmem(8),
    )(rhs, mine, other, core)


def sum_kernel(shares_ref, panel_ref, trail_ref, solved_ref, low_ref):
    height = shares_ref.shape[1] - 8
    scale = jnp.exp2(shares_ref[:, height:] - TOP)
    total = jnp.concatenate(
        [jnp.sum(shares_ref[:, i : i + 8] * scale, axis=0) for i in range(0, height, 8)], axis=0
    )
    solved_ref[...] = total
    low_ref[...] = jnp.broadcast_to(total.astype(jnp.bfloat16)[None], low_ref.shape)


def summed(shares, copies, panel, trail):
    height, width = shares.shape[1] - 8, shares.shape[2]
    return pl.pallas_call(
        sum_kernel,
        out_shape=(
            jax.ShapeDtypeStruct((height, width), jnp.float32),
            jax.ShapeDtypeStruct((copies, height, width), jnp.bfloat16),
        ),
        compiler_params=vmem(8),
    )(shares, panel, trail)


def stripes_kernel(core_ref, tiles_ref, panel_ref, trail_ref, passed_ref, out_ref, *rest):
    yn = pl.program_id(0)
    _, near_z, _, far_y, far_z, far_x, _, _ = tiles_ref.shape
    rows = []
    for y in range(far_y):
        pairs = [
            crossed(tiles_ref[yn, n, 0, y, z, x], tiles_ref[yn, n, 1, y, z, x])
            for z in range(far_z)
            for n in range(near_z)
            for x in range(far_x)
        ]
        rows += [jnp.concatenate([p[h] for p in pairs], axis=1) for h in range(2)]
    update = jnp.dot(jnp.concatenate(rows, axis=0), panel_ref[...], preferred_element_type=jnp.float32)
    out_ref[:, 0, 0] = trail_ref[:, yn, core_ref[0]] - update.reshape(far_y, -1, update.shape[1])
    for solved_ref in rest:
        both, (count, half) = passed_ref[...], passed_ref.shape
        solved_ref[:count] = both[:, : half // 2]
        solved_ref[count:] = pltpu.roll(both, half // 2, 1)[:, : half // 2]


def updated_stripes(tiles, panel, trail, core, solved=None, done=None):
    near_y, far_y, height = tiles.shape[0], tiles.shape[3], tiles.shape[6]
    columns = panel.shape[1]
    stripe = pl.BlockSpec((far_y, 1, 1, 2 * height, columns), lambda i, core: (0, i, core[0], 0, 0))
    whole = pl.BlockSpec(memory_space=pltpu.VMEM)
    flops = 2 * near_y * far_y * 2 * height * panel.shape[0] * columns
    out = jax.ShapeDtypeStruct(trail.shape, jnp.float32)
    if solved is not None:
        tile = (2 * solved.shape[0], solved.shape[1] // 2)
        block, unpacked = (pl.BlockSpec(shape, lambda i, core: (0, 0)) for shape in (solved.shape, tile))
    return pl.pallas_call(
        stripes_kernel,
        out_shape=out if solved is None else (out, jax.ShapeDtypeStruct(tile, solved.dtype)),
        grid_spec=pltpu.PrefetchScalarGridSpec(
            num_scalar_prefetch=1,
            grid=(near_y,),
            in_specs=[whole, whole, whole, pl.BlockSpec(memory_space=pl.ANY) if solved is None else block],
            out_specs=stripe if solved is None else (stripe, unpacked),
        ),
        input_output_aliases={4: 0} if solved is None else {},
        compiler_params=vmem(20),
        cost_estimate=pl.CostEstimate(flops=flops, bytes_accessed=5 * 1024 * 1024, transcendentals=0),
    )(core, tiles, panel, trail, done if solved is None else solved)


def cubes(size):
    count_y, count_z, count_x = 2 * size["yf"], 2 * size["zf"], 2 * size["xf"]

    def device(y, core, z, x):
        return ((y % count_y * size["core"] + core) * count_z + z % count_z) * count_x + x % count_x

    def place(corner, parity, core):
        return corner + (2 - parity if core else parity)

    return [
        [
            device(place(y, b, core), core, place(z, a, core), place(x, c, core))
            for a in range(2)
            for b in range(2)
            for c in range(2)
        ]
        for y in range(0, count_y, 2)
        for core in range(size["core"])
        for z in range(0, count_z, 2)
        for x in range(0, count_x, 2)
    ]


def local(size, rhs_block, diag_inverse, panel, rhs_trail):
    core = lax.axis_index("core").reshape(1)
    other_inverse = lax.ppermute(diag_inverse, "core", SWAP)
    half, count_y, count_z = rhs_block.shape[0] // 2, size["yf"] * size["yn"], size["zf"] * size["zn"]
    shape = (count_y, half, rhs_block.shape[1])
    rows = [jnp.broadcast_to(part[None], shape) for part in (rhs_block[:half], rhs_block[half:])]
    rows = lax.all_to_all(jnp.concatenate(rows, axis=2), ("yf", "yn"), 0, 0, tiled=True)
    blocks = partial_blocks(rows, diag_inverse, other_inverse, core).astype(jnp.float16)
    shares = lax.all_to_all(blocks, COL, 0, 0, tiled=True)
    trail = rhs_trail.reshape(size["zf"], size["zn"], 2, 2 * half, rhs_trail.shape[1])
    solved, low = summed(shares.astype(jnp.float32), size["yf"] * size["zf"] * size["xf"], panel, trail)
    count_x = size["xf"] * size["xn"]
    swapped = [
        (((y * 2 + k) * count_z + z) * count_x + x, ((z * 2 + k) * count_y + y) * count_x + x)
        for y in range(count_y)
        for k in range(2)
        for z in range(count_z)
        for x in range(count_x)
    ]
    solved = lax.ppermute(solved, ROW + COL, swapped)
    far, solved = lax.optimization_barrier((lax.all_to_all(low, FAR, 0, 0, tiled=True), solved))
    copies = size["yn"] * size["zn"] * size["xn"]
    near = lax.all_to_all(
        jnp.broadcast_to(far[None], (copies,) + far.shape), ROW + COL, 0, 0, tiled=True, axis_index_groups=cubes(size)
    )
    tiles = near.reshape(tuple(size[a] for a in NEAR + FAR) + far.shape[1:])
    other = lax.ppermute(tiles, "core", SWAP)
    done, solved = updated_stripes(tiles, panel, trail, core, solved=solved)
    done = updated_stripes(other, panel, trail, 1 - core, done=done)
    return solved, done.reshape(rhs_trail.shape)


def solution(mesh):
    split = Mesh(mesh.devices.reshape(4, 2, 2, 4, 2, 2, 2), ROW + COL)
    return jax.shard_map(
        functools.partial(local, dict(split.shape)),
        mesh=split,
        in_specs=(P(ROW, COL), P(COL, ROW), P(None, ROW + COL), P(None, ROW + COL)),
        out_specs=(P(ROW, COL), P(None, ROW + COL)),
        check_vma=False,
    )
```

```python
import functools

import jax
import jax.numpy as jnp
from jax import lax
from jax.experimental import pallas as pl
from jax.experimental.pallas import tpu as pltpu
from jax.sharding import Mesh, PartitionSpec as P

ROW = ("yf", "yn", "core")
COL = ("zf", "zn", "xf", "xn")
FAR = ("zf", "yf", "xf")
NEAR = ("zn", "yn", "xn")
SWAP = [(0, 1), (1, 0)]
TOP = 15.0


def vmem(mib):
    return pltpu.CompilerParams(vmem_limit_bytes=mib * 1024 * 1024)


def crossed(top, bottom):
    half = top.shape[1] // 2
    first = lax.broadcasted_iota(jnp.int32, top.shape, 1) < half
    return (
        jnp.where(first, top, pltpu.roll(bottom, half, 1)),
        jnp.where(first, pltpu.roll(top, half, 1), bottom),
    )


def partial_kernel(rhs_ref, mine_ref, other_ref, core_ref, out_ref, here_ref, sem):
    copy = pltpu.make_async_copy(mine_ref, here_ref, sem)
    copy.start()
    count, height, half = rhs_ref.shape[0], rhs_ref.shape[1], rhs_ref.shape[2] // 2
    rows = []
    for i in range(count):
        both = rhs_ref[i]
        rows += [both[:, :half], pltpu.roll(both, half, 1)[:, :half]]
    first = core_ref[0] == 0
    copy.wait()
    mine, other = here_ref[...], other_ref[...]
    inverse = jnp.concatenate([jnp.where(first, mine, other), jnp.where(first, other, mine)], axis=1)
    partial = jnp.dot(
        jnp.concatenate(rows, axis=0), inverse, preferred_element_type=jnp.float32, precision=lax.Precision.HIGHEST
    )
    largest = jnp.maximum(jnp.max(jnp.abs(partial), axis=(0, 1), keepdims=True), 2.0**-100)
    power = jnp.ceil(jnp.log2(largest))
    partial = partial * jnp.exp2(TOP - power)
    block = 0
    for i in range(count):
        for j in range(partial.shape[1] // 128):
            both = partial[2 * height * i : 2 * height * (i + 1), 128 * j : 128 * (j + 1)]
            out_ref[block, :height], out_ref[block + 1, :height] = crossed(both[:height], both[height:])
            block += 2
    out_ref[:, height:] = jnp.broadcast_to(power[None], (out_ref.shape[0], 8, 128))


def partial_blocks(rhs, mine, other, core):
    count, height, _ = rhs.shape
    whole = pl.BlockSpec(memory_space=pltpu.VMEM)
    return pl.pallas_call(
        partial_kernel,
        out_shape=jax.ShapeDtypeStruct((count * 2 * mine.shape[1] // 64, height + 8, 128), jnp.float32),
        in_specs=[whole, pl.BlockSpec(memory_space=pltpu.HBM), whole, pl.BlockSpec(memory_space=pltpu.SMEM)],
        scratch_shapes=[pltpu.VMEM(mine.shape, mine.dtype), pltpu.SemaphoreType.DMA],
        compiler_params=vmem(8),
    )(rhs, mine, other, core)


def sum_kernel(shares_ref, panel_ref, trail_ref, solved_ref, low_ref):
    height = shares_ref.shape[1] - 8
    scale = jnp.exp2(shares_ref[:, height:] - TOP)
    total = jnp.concatenate(
        [jnp.sum(shares_ref[:, i : i + 8] * scale, axis=0) for i in range(0, height, 8)], axis=0
    )
    solved_ref[...] = total
    low_ref[...] = jnp.broadcast_to(total.astype(jnp.bfloat16)[None], low_ref.shape)


def summed(shares, copies, panel, trail):
    height, width = shares.shape[1] - 8, shares.shape[2]
    return pl.pallas_call(
        sum_kernel,
        out_shape=(
            jax.ShapeDtypeStruct((height, width), jnp.float32),
            jax.ShapeDtypeStruct((copies, height, width), jnp.bfloat16),
        ),
        compiler_params=vmem(8),
    )(shares, panel, trail)


def stripes_kernel(core_ref, tiles_ref, panel_ref, trail_ref, passed_ref, out_ref, *rest):
    yn = pl.program_id(0)
    _, near_z, _, far_y, far_z, far_x, _, _ = tiles_ref.shape
    rows = []
    for y in range(far_y):
        pairs = [
            crossed(tiles_ref[yn, n, 0, y, z, x], tiles_ref[yn, n, 1, y, z, x])
            for z in range(far_z)
            for n in range(near_z)
            for x in range(far_x)
        ]
        rows += [jnp.concatenate([p[h] for p in pairs], axis=1) for h in range(2)]
    update = jnp.dot(jnp.concatenate(rows, axis=0), panel_ref[...], preferred_element_type=jnp.float32)
    out_ref[:, 0, 0] = trail_ref[:, yn, core_ref[0]] - update.reshape(far_y, -1, update.shape[1])
    for solved_ref in rest:
        both, (count, half) = passed_ref[...], passed_ref.shape
        solved_ref[:count] = both[:, : half // 2]
        solved_ref[count:] = pltpu.roll(both, half // 2, 1)[:, : half // 2]


def updated_stripes(tiles, panel, trail, core, solved=None, done=None):
    near_y, far_y, height = tiles.shape[0], tiles.shape[3], tiles.shape[6]
    columns = panel.shape[1]
    stripe = pl.BlockSpec((far_y, 1, 1, 2 * height, columns), lambda i, core: (0, i, core[0], 0, 0))
    whole = pl.BlockSpec(memory_space=pltpu.VMEM)
    flops = 2 * near_y * far_y * 2 * height * panel.shape[0] * columns
    out = jax.ShapeDtypeStruct(trail.shape, jnp.float32)
    if solved is not None:
        tile = (2 * solved.shape[0], solved.shape[1] // 2)
        block, unpacked = (pl.BlockSpec(shape, lambda i, core: (0, 0)) for shape in (solved.shape, tile))
    return pl.pallas_call(
        stripes_kernel,
        out_shape=out if solved is None else (out, jax.ShapeDtypeStruct(tile, solved.dtype)),
        grid_spec=pltpu.PrefetchScalarGridSpec(
            num_scalar_prefetch=1,
            grid=(near_y,),
            in_specs=[whole, whole, whole, pl.BlockSpec(memory_space=pl.ANY) if solved is None else block],
            out_specs=stripe if solved is None else (stripe, unpacked),
        ),
        input_output_aliases={4: 0} if solved is None else {},
        compiler_params=vmem(20),
        cost_estimate=pl.CostEstimate(flops=flops, bytes_accessed=5 * 1024 * 1024, transcendentals=0),
    )(core, tiles, panel, trail, done if solved is None else solved)


def cubes(size):
    count_y, count_z, count_x = 2 * size["yf"], 2 * size["zf"], 2 * size["xf"]

    def device(y, core, z, x):
        return ((y % count_y * size["core"] + core) * count_z + z % count_z) * count_x + x % count_x

    def place(corner, parity, core):
        return corner + (2 - parity if core else parity)

    return [
        [
            device(place(y, b, core), core, place(z, a, core), place(x, c, core))
            for a in range(2)
            for b in range(2)
            for c in range(2)
        ]
        for y in range(0, count_y, 2)
        for core in range(size["core"])
        for z in range(0, count_z, 2)
        for x in range(0, count_x, 2)
    ]


def local(size, rhs_block, diag_inverse, panel, rhs_trail):
    core = lax.axis_index("core").reshape(1)
    other_inverse = lax.ppermute(diag_inverse, "core", SWAP)
    half, count_y, count_z = rhs_block.shape[0] // 2, size["yf"] * size["yn"], size["zf"] * size["zn"]
    shape = (count_y, half, rhs_block.shape[1])
    rows = [jnp.broadcast_to(part[None], shape) for part in (rhs_block[:half], rhs_block[half:])]
    rows = lax.all_to_all(jnp.concatenate(rows, axis=2), ("yf", "yn"), 0, 0, tiled=True)
    blocks = partial_blocks(rows, diag_inverse, other_inverse, core).astype(jnp.float16)
    shares = lax.all_to_all(blocks, COL, 0, 0, tiled=True)
    trail = rhs_trail.reshape(size["zf"], size["zn"], 2, 2 * half, rhs_trail.shape[1])
    solved, low = summed(shares.astype(jnp.float32), size["yf"] * size["zf"] * size["xf"], panel, trail)
    count_x = size["xf"] * size["xn"]
    swapped = [
        (((y * 2 + k) * count_z + z) * count_x + x, ((z * 2 + k) * count_y + y) * count_x + x)
        for y in range(count_y)
        for k in range(2)
        for z in range(count_z)
        for x in range(count_x)
    ]
    solved = lax.ppermute(solved, ROW + COL, swapped)
    far, solved = lax.optimization_barrier((lax.all_to_all(low, FAR, 0, 0, tiled=True), solved))
    copies = size["yn"] * size["zn"] * size["xn"]
    near = lax.all_to_all(
        jnp.broadcast_to(far[None], (copies,) + far.shape), ROW + COL, 0, 0, tiled=True, axis_index_groups=cubes(size)
    )
    tiles = near.reshape(tuple(size[a] for a in NEAR + FAR) + far.shape[1:])
    other = lax.ppermute(tiles, "core", SWAP)
    done, solved = updated_stripes(tiles, panel, trail, core, solved=solved)
    done = updated_stripes(other, panel, trail, 1 - core, done=done)
    return solved, done.reshape(rhs_trail.shape)


def solution(mesh):
    split = Mesh(mesh.devices.reshape(4, 2, 2, 4, 2, 2, 2), ROW + COL)
    return jax.shard_map(
        functools.partial(local, dict(split.shape)),
        mesh=split,
        in_specs=(P(ROW, COL), P(COL, ROW), P(None, ROW + COL), P(None, ROW + COL)),
        out_specs=(P(ROW, COL), P(None, ROW + COL)),
        check_vma=False,
    )
```
